32 devices in a mesh: seq: 8 (over z, y), head: 4 (over x, core).
Axes of the slice: x: 2, y: 2, z: 4, core: 2. Of those that a mesh axis runs over, the one named last changes fastest.
Arguments:
- tokens: bfloat16 [2, 4096, 1024], P(None, 'seq'), may hold values from -6 to 6
- norm_gain: bfloat16 [1024], P('seq'), may hold values from 0.5 to 1.5
- qk_proj: bfloat16 [1024, 2, 8, 128], P('seq', None, 'head'), may hold values from -0.1875 to 0.1875
- vg_proj: bfloat16 [1024, 2, 8, 256], P('seq', None, 'head'), may hold values from -0.1875 to 0.1875
- ab_proj: bfloat16 [1024, 2, 8], P('seq', None, 'head'), may hold values from -0.1875 to 0.1875
- qk_conv: bfloat16 [4, 2, 8, 128], P(None, None, 'head', 'seq'), may hold values from -3 to 3
- v_conv: bfloat16 [4, 8, 256], P(None, 'head', 'seq'), may hold values from -3 to 3
- decay_terms: float32 [2, 8], P(None, 'head'), may hold values from -9 to 1, as said below
- out_gain: bfloat16 [256], P('seq'), may hold values from 0.5 to 1.5
- out_proj: bfloat16 [8, 256, 1024], P('head', None, 'seq'), may hold values from -0.1875 to 0.1875
- ffn_gain: bfloat16 [1024], P('seq'), may hold values from 0.5 to 1.5
- gate_up: bfloat16 [1024, 2, 2816], P('seq', None, 'head'), may hold values from -0.1875 to 0.1875
- down_proj: bfloat16 [2816, 1024], P('head', 'seq'), may hold values from -0.21875 to 0.21875
- cotangent: bfloat16 [2, 4096, 1024], P(None, 'seq'), may hold values from -6 to 6
Outputs:
- block_out: bfloat16 [2, 4096, 1024], P(None, 'seq')
- tokens_grad: float32 [2, 4096, 1024], P(None, 'seq')
- norm_gain_grad: float32 [1024], P('seq')
- qk_proj_grad: float32 [1024, 2, 8, 128], P('seq', None, 'head')
- vg_proj_grad: float32 [1024, 2, 8, 256], P('seq', None, 'head')
- ab_proj_grad: float32 [1024, 2, 8], P('seq', None, 'head')
- qk_conv_grad: float32 [4, 2, 8, 128], P(None, None, 'head', 'seq')
- v_conv_grad: float32 [4, 8, 256], P(None, 'head', 'seq')
- decay_grad: float32 [2, 8], P(None, 'head')
- out_gain_grad: float32 [256], P('seq')
- out_proj_grad: float32 [8, 256, 1024], P('head', None, 'seq')
- ffn_gain_grad: float32 [1024], P('seq')
- gate_up_grad: float32 [1024, 2, 2816], P('seq', None, 'head')
- down_proj_grad: float32 [2816, 1024], P('head', 'seq')
The draws below stay inside these ranges and needn't reach their ends.
Inputs may be any that keep to these rules, and one draw needn't show every extreme that they name: decay_terms row 0 lies in -1 to 1 and row 1 in -9 to -3.
All inputs are finite; a program needn't handle non-finite values.
Results may differ from the reference program's by a relative error of at most 0.011.
Values may be sent and summed in bfloat16 or wider, within the bound.
A program may use at most 256 MiB of HBM per device.

```python
import jax
import jax.numpy as jnp
from jax import lax

D = 1024
H = 8
DK = 128
DV = 256
FF = 2816
CONV = 4
SPAN = 64
SEQS = 2
L = 4096


def draw_decay_terms(key, part):
    key = jax.random.fold_in(key, 11)
    rate_key, bias_key = jax.random.split(key)
    log_rates = jax.random.uniform(rate_key, (H,), jnp.float32, -1.0, 1.0)
    biases = jax.random.uniform(bias_key, (H,), jnp.float32, -9.0, -3.0)
    return jnp.stack([log_rates, biases], 0)


def shard_levels(rng, shape, pieces, low, largest):
    def one(dim, shards_of):
        steps = jax.random.uniform(jax.random.fold_in(jax.random.fold_in(rng, 6), dim), (shards_of,), jnp.float32, low / len(pieces), largest / len(pieces))
        return jnp.repeat(jnp.exp(steps), shape[dim] // shards_of).reshape((-1,) + (1,) * (len(shape) - dim - 1))

    level = one(*pieces[0])
    for cut in pieces[1:]:
        level = level * one(*cut)
    return level


def normal_values(key, shape, scale, bound, cuts=(), kind=jnp.bfloat16):
    result = jax.random.normal(key, shape, jnp.float32) * scale
    if len(cuts) > 0:
        result = shard_levels(key, shape, cuts, -0.22, 0.18) * result
    return jnp.clip(result, min=-bound, max=bound).astype(kind)


def setup_inputs(seed: int = 0) -> dict:
    key_of = jax.random.split(jax.random.key(seed), 15)
    tokens = normal_values(key_of[0], (SEQS, L, D), 1.0, 6.0, ((1, 8),))
    norm_gain = jnp.clip(1.0 + 0.1 * jax.random.normal(key_of[1], (D,), jnp.float32), 0.5, 1.5).astype(jnp.bfloat16)
    qk_proj = normal_values(key_of[2], (D, 2, H, DK), D ** -0.5, 0.1875, ((0, 8), (2, 4)))
    vg_proj = normal_values(key_of[3], (D, 2, H, DV), D ** -0.5, 0.1875, ((0, 8), (2, 4)))
    ab_proj = normal_values(key_of[4], (D, 2, H), D ** -0.5, 0.1875, ((0, 8), (2, 4)))
    qk_conv = normal_values(key_of[5], (CONV, 2, H, DK), CONV ** -0.5, 3.0, ((2, 4), (3, 8)))
    v_conv = normal_values(key_of[6], (CONV, H, DV), CONV ** -0.5, 3.0, ((1, 4), (2, 8)))
    decay_terms = draw_decay_terms(jax.random.fold_in(key_of[14], 71), 0)
    out_gain = jnp.clip(1.0 + 0.1 * jax.random.normal(key_of[8], (DV,), jnp.float32), 0.5, 1.5).astype(jnp.bfloat16)
    out_proj = normal_values(key_of[9], (H, DV, D), (H * DV // 2) ** -0.5, 0.1875, ((0, 4), (2, 8)))
    ffn_gain = jnp.clip(1.0 + 0.1 * jax.random.normal(key_of[10], (D,), jnp.float32), 0.5, 1.5).astype(jnp.bfloat16)
    gate_up = normal_values(key_of[11], (D, 2, FF), D ** -0.5, 0.1875, ((0, 8), (2, 4)))
    down_proj = normal_values(key_of[12], (FF, D), (FF // 4) ** -0.5, 0.21875, ((0, 4), (1, 8)))
    cotangent = normal_values(key_of[13], (SEQS, L, D), 1.0, 6.0, ((1, 8),))
    return dict(tokens=tokens, norm_gain=norm_gain, qk_proj=qk_proj, vg_proj=vg_proj, ab_proj=ab_proj, qk_conv=qk_conv, v_conv=v_conv, decay_terms=decay_terms, out_gain=out_gain, out_proj=out_proj, ffn_gain=ffn_gain, gate_up=gate_up, down_proj=down_proj, cotangent=cotangent)


HIGHEST = lax.Precision.HIGHEST

@jax.custom_vjp
def low(v):
    return lax.optimization_barrier(v.astype(jnp.bfloat16)).astype(jnp.float32)

@jax.custom_vjp
def low_back(v):
    return v

def low_keep(v):
    return (low(v), None)

def low_pass(kept, grad):
    return (grad,)

def back_keep(v):
    return (v, None)

def back_low(kept, grad):
    return (low(grad),)
low.defvjp(low_keep, low_pass)
low_back.defvjp(back_keep, back_low)

def product(first_op, second_op):
    return jnp.matmul(first_op, second_op, precision=HIGHEST)

def flip(matrix):
    return jnp.swapaxes(matrix, -1, -2)

def inverse_unit(strict):
    span_len = strict.shape[-1]
    identity = jnp.eye(span_len, dtype=jnp.float32)
    inverse = identity - strict
    powered = strict
    reached = 2
    while reached < span_len:
        powered = product(powered, powered)
        inverse = product(inverse, identity + powered)
        reached = reached * 2
    return inverse

def span_parts(queries, key_rows, value_rows, beta_rows, log_decay):
    span_len = queries.shape[-2]
    cumulative = jnp.cumsum(log_decay, -1)
    spread = cumulative[..., :, None] - cumulative[..., None, :]
    lower_tri = jnp.tril(jnp.ones((span_len, span_len), jnp.float32))
    below_diag = lower_tri - jnp.eye(span_len, dtype=jnp.float32)
    ratios = lower_tri * jnp.exp(jnp.where(lower_tri > 0, spread, 0.0))
    key_gram = product(key_rows, flip(key_rows))
    strict = beta_rows[..., :, None] * ratios * key_gram * below_diag
    inverse = inverse_unit(strict)
    decayed = jnp.exp(cumulative)
    writes = product(inverse, (beta_rows * decayed)[..., None] * key_rows)
    pseudo = product(inverse, beta_rows[..., None] * value_rows)
    scores = ratios * product(queries, flip(key_rows))
    intra_out = product(scores, pseudo)
    read_map = decayed[..., None] * queries - product(scores, writes)
    tail_decay = jnp.exp(cumulative[..., -1:] - cumulative)
    tail_keys = tail_decay[..., None] * key_rows
    key_eye = jnp.eye(key_rows.shape[-1], dtype=jnp.float32)
    carry_map = decayed[..., -1][..., None, None] * key_eye - product(flip(tail_keys), writes)
    carry_add = product(flip(tail_keys), pseudo)
    return (carry_map, carry_add, read_map, intra_out)

def conv_valid(extended, weights):
    tap_count = weights.shape[0]
    seq_len = extended.shape[1] - tap_count + 1
    summed = weights[0] * extended[:, 0:seq_len]
    for tap_idx in range(1, tap_count):
        summed = summed + weights[tap_idx] * extended[:, tap_idx:tap_idx + seq_len]
    return summed

def unit_rows(values):
    return values * lax.rsqrt(lax.optimization_barrier(jnp.sum(values * values, -1, keepdims=True)) + 1e-06)

def normalize(values, gain_vec, epsilon):
    return values * lax.rsqrt(lax.optimization_barrier(jnp.mean(values * values, -1, keepdims=True)) + epsilon) * gain_vec

def input_norm(values, gain_vec):
    return normalize(values, gain_vec, 1e-06)

def output_norm(mixer_out, gate_pre, gain_vec):
    return normalize(mixer_out, gain_vec, 1e-05) * jax.nn.silu(gate_pre)

def swiglu(gu_pre):
    return jax.nn.silu(gu_pre[:, :, 0]) * gu_pre[:, :, 1]

def mixer_inputs(qk_ext, v_ext, ab_pre, qk_taps, v_taps, decay_terms):
    qk_act = jax.nn.silu(conv_valid(qk_ext, qk_taps))
    queries = unit_rows(qk_act[:, :, 0]) * qk_act.shape[-1] ** (-0.5)
    key_rows = unit_rows(qk_act[:, :, 1])
    value_rows = jax.nn.silu(conv_valid(v_ext, v_taps))
    beta_rows = jax.nn.sigmoid(ab_pre[:, :, 1])
    log_decay = -jnp.exp(decay_terms[0]) * jax.nn.softplus(ab_pre[:, :, 0] + decay_terms[1])
    return (queries, key_rows, value_rows, beta_rows, log_decay)

def pad_front(values, pad_width):
    return jnp.pad(values, ((0, 0), (pad_width, 0)) + ((0, 0),) * (values.ndim - 2))

def mixer(queries, key_rows, value_rows, beta_rows, log_decay):
    num_seqs, seq_len, num_heads = queries.shape[:3]
    blocks = seq_len // SPAN

    def to_blocks(tensor):
        shaped = tensor.reshape((num_seqs, blocks, SPAN) + tensor.shape[2:])
        return jnp.swapaxes(jnp.moveaxis(shaped, 1, 0), 2, 3)

    def advance(carried, inputs):
        query_blk, key_blk, value_blk, beta_blk, decay_blk = inputs
        carry_map, carry_add, read_map, intra_out = span_parts(query_blk, key_blk, value_blk, beta_blk, decay_blk)
        output = intra_out + product(read_map, carried)
        return (product(carry_map, carried) + carry_add, output)
    initial = jnp.zeros((num_seqs, num_heads, key_rows.shape[-1], value_rows.shape[-1]), jnp.float32)
    blocked = (to_blocks(queries), to_blocks(key_rows), to_blocks(value_rows), to_blocks(beta_rows), to_blocks(log_decay))
    final_state, outputs = lax.scan(jax.checkpoint(advance), initial, blocked)
    outputs = jnp.moveaxis(jnp.swapaxes(outputs, 2, 3), 0, 1)
    return outputs.reshape((num_seqs, seq_len, num_heads, value_rows.shape[-1]))

def forward(tok_float, norm_gain, qk_proj, vg_proj, ab_proj, qk_conv, v_conv, decay_terms, out_gain, out_proj, ffn_gain, gate_up, down_proj):
    normed = low(input_norm(tok_float, norm_gain))
    qk_pre = low_back(jnp.einsum('bld,dphe->blphe', normed, qk_proj, precision=HIGHEST))
    vg_pre = low_back(jnp.einsum('bld,dphe->blphe', normed, vg_proj, precision=HIGHEST))
    ab_pre = low_back(jnp.einsum('bld,dph->blph', normed, ab_proj, precision=HIGHEST))
    pad_width = qk_conv.shape[0] - 1
    qk_ext = pad_front(qk_pre, pad_width)
    v_ext = pad_front(vg_pre[:, :, 0], pad_width)
    queries, key_rows, value_rows, beta_rows, log_decay = mixer_inputs(qk_ext, v_ext, ab_pre, qk_conv, v_conv, decay_terms)
    mixer_out = mixer(queries, key_rows, value_rows, beta_rows, log_decay)
    gated_out = low(output_norm(mixer_out, vg_pre[:, :, 1], out_gain))
    mix_sum = low_back(jnp.einsum('blhe,hed->bld', gated_out, out_proj, precision=HIGHEST))
    hidden_res = tok_float + mix_sum
    normed_ffn = low(input_norm(hidden_res, ffn_gain))
    gu_pre = low_back(jnp.einsum('bld,dpf->blpf', normed_ffn, gate_up, precision=HIGHEST))
    activated = low(swiglu(gu_pre))
    ffn_out = low_back(jnp.einsum('blf,fd->bld', activated, down_proj, precision=HIGHEST))
    return hidden_res + ffn_out

def reference(tokens, norm_gain, qk_proj, vg_proj, ab_proj, qk_conv, v_conv, decay_terms, out_gain, out_proj, ffn_gain, gate_up, down_proj, cotangent):
    params = tuple((array_in.astype(jnp.float32) for array_in in (tokens, norm_gain, qk_proj, vg_proj, ab_proj, qk_conv, v_conv, decay_terms, out_gain, out_proj, ffn_gain, gate_up, down_proj)))
    block_out, pullback = jax.vjp(forward, *params)
    grads = pullback(cotangent.astype(jnp.float32))
    return (block_out.astype(jnp.bfloat16), grads[0], grads[1], grads[2], grads[3], grads[4], grads[5], grads[6], grads[7], grads[8], grads[9], grads[10], grads[11], grads[12])
```

```python
import jax
import jax.numpy as jnp
from jax import lax
from jax.sharding import PartitionSpec as P

SPAN = 64


HIGH = lax.Precision.HIGH


def from_behind(x, axis, by):
    peers = lax.axis_size(axis)
    pairs = [(i, i + by) for i in range(peers) if 0 <= i + by < peers]
    return lax.ppermute(x, axis, pairs)


def product(first_op, second_op):
    return jnp.matmul(first_op, second_op, precision=HIGH)


def flip(matrix):
    return jnp.swapaxes(matrix, -1, -2)


def inverse_unit(strict):
    span_len = strict.shape[-1]
    identity = jnp.eye(span_len, dtype=jnp.float32)
    inverse = identity - strict
    powered = strict
    reached = 2
    while reached < span_len:
        powered = product(powered, powered)
        inverse = product(inverse, identity + powered)
        reached = reached * 2
    return inverse


def span_parts(queries, key_rows, value_rows, beta_rows, log_decay):
    span_len = queries.shape[-2]
    cumulative = jnp.cumsum(log_decay, -1)
    spread = cumulative[..., :, None] - cumulative[..., None, :]
    lower_tri = jnp.tril(jnp.ones((span_len, span_len), jnp.float32))
    below_diag = lower_tri - jnp.eye(span_len, dtype=jnp.float32)
    ratios = lower_tri * jnp.exp(jnp.where(lower_tri > 0, spread, 0.0))
    key_gram = product(key_rows, flip(key_rows))
    strict = beta_rows[..., :, None] * ratios * key_gram * below_diag
    inverse = inverse_unit(strict)
    decayed = jnp.exp(cumulative)
    writes = product(inverse, (beta_rows * decayed)[..., None] * key_rows)
    pseudo = product(inverse, beta_rows[..., None] * value_rows)
    scores = ratios * product(queries, flip(key_rows))
    intra_out = product(scores, pseudo)
    read_map = decayed[..., None] * queries - product(scores, writes)
    tail_decay = jnp.exp(cumulative[..., -1:] - cumulative)
    tail_keys = tail_decay[..., None] * key_rows
    key_eye = jnp.eye(key_rows.shape[-1], dtype=jnp.float32)
    carry_map = decayed[..., -1][..., None, None] * key_eye - product(flip(tail_keys), writes)
    carry_add = product(flip(tail_keys), pseudo)
    return (carry_map, carry_add, read_map, intra_out)


def conv_valid(extended, weights):
    tap_count = weights.shape[0]
    seq_len = extended.shape[1] - tap_count + 1
    summed = weights[0] * extended[:, 0:seq_len]
    for tap_idx in range(1, tap_count):
        summed = summed + weights[tap_idx] * extended[:, tap_idx : tap_idx + seq_len]
    return summed


def unit_rows(values):
    return values * lax.rsqrt(jnp.sum(values * values, -1, keepdims=True) + 1e-06)


def normalize(values, gain_vec, epsilon):
    return values * lax.rsqrt(jnp.mean(values * values, -1, keepdims=True) + epsilon) * gain_vec


def input_norm(values, gain_vec):
    return normalize(values, gain_vec, 1e-06)


def output_norm(mixer_out, gate_pre, gain_vec):
    return normalize(mixer_out, gain_vec, 1e-05) * jax.nn.silu(gate_pre)


def swiglu(gu_pre):
    return jax.nn.silu(gu_pre[:, :, 0]) * gu_pre[:, :, 1]


def mixer_inputs(qk_ext, v_ext, ab_pre, qk_taps, v_taps, decay_terms):
    qk_act = jax.nn.silu(conv_valid(qk_ext, qk_taps))
    queries = unit_rows(qk_act[:, :, 0]) * qk_act.shape[-1] ** (-0.5)
    key_rows = unit_rows(qk_act[:, :, 1])
    value_rows = jax.nn.silu(conv_valid(v_ext, v_taps))
    beta_rows = jax.nn.sigmoid(ab_pre[:, :, 1])
    log_decay = -jnp.exp(decay_terms[0]) * jax.nn.softplus(ab_pre[:, :, 0] + decay_terms[1])
    return (queries, key_rows, value_rows, beta_rows, log_decay)


def to_spans(tensor):
    shaped = tensor.reshape((tensor.shape[0], tensor.shape[1] // SPAN, SPAN) + tensor.shape[2:])
    return jnp.moveaxis(shaped, 3, 1)


def from_spans(tensor):
    shaped = jnp.moveaxis(tensor, 1, 3)
    return shaped.reshape((shaped.shape[0], shaped.shape[1] * shaped.shape[2]) + shaped.shape[3:])


def prepare(qk_ext, v_ext, ab_pre, qk_taps, v_taps, decay_terms):
    queries, key_rows, value_rows, beta_rows, log_decay = mixer_inputs(
        qk_ext, v_ext, ab_pre, qk_taps, v_taps, decay_terms
    )
    return span_parts(
        to_spans(queries),
        to_spans(key_rows),
        to_spans(value_rows),
        to_spans(beta_rows),
        to_spans(log_decay),
    )


def finish(span_terms, state_in):
    carry_map, carry_add, read_map, intra_out = span_terms
    carried = state_in
    states = []
    for span_idx in range(carry_map.shape[2]):
        states.append(carried)
        carried = product(carry_map[:, :, span_idx], carried) + carry_add[:, :, span_idx]
    stacked = jnp.stack(states, 2)
    return (from_spans(intra_out + product(read_map, stacked)), carried)


def compose(span_terms):
    carry_map, carry_add = (span_terms[0], span_terms[1])
    whole_map = carry_map[:, :, 0]
    whole_add = carry_add[:, :, 0]
    for span_idx in range(1, carry_map.shape[2]):
        whole_map = product(carry_map[:, :, span_idx], whole_map)
        whole_add = product(carry_map[:, :, span_idx], whole_add) + carry_add[:, :, span_idx]
    return (whole_map, whole_add)


def head_rows(values, count):
    mine = lax.axis_index("head")
    return lax.dynamic_slice_in_dim(values, mine * count, count, 1)


def per_device(
    tokens,
    norm_gain,
    qk_proj,
    vg_proj,
    ab_proj,
    qk_conv,
    v_conv,
    decay_terms,
    out_gain,
    out_proj,
    ffn_gain,
    gate_up,
    down_proj,
    cotangent,
):
    f32, bf16 = jnp.float32, jnp.bfloat16
    peers = lax.axis_size("seq")
    head_peers = lax.axis_size("head")
    rows, width = norm_gain.shape[0], norm_gain.shape[0] * peers
    taps, _, heads, dk_part = qk_conv.shape
    dv_part = v_conv.shape[2]
    dk, dv = qk_proj.shape[3], vg_proj.shape[3]
    hidden = gate_up.shape[2]
    seqs, seq_len = tokens.shape[:2]
    quarter = seq_len // head_peers
    qk_n, vg_n, ab_n = 2 * heads * dk, 2 * heads * dv, 2 * heads

    small = jnp.concatenate([qk_conv.reshape(-1), v_conv.reshape(-1), out_gain])
    small_n = small.shape[0]
    small_cols = -(-small_n // rows)
    small = jnp.pad(small, (0, small_cols * rows - small_n)).reshape(rows, small_cols)
    used = qk_n + vg_n + ab_n + 2 + small_cols
    spare = -used % 128
    first_local = jnp.concatenate(
        [
            qk_proj.reshape(rows, qk_n),
            vg_proj.reshape(rows, vg_n),
            ab_proj.reshape(rows, ab_n),
            norm_gain[:, None],
            ffn_gain[:, None],
            small,
            jnp.zeros((rows, spare), bf16),
        ],
        1,
    )
    first = lax.all_gather(first_local, "seq", axis=0, tiled=True)
    mix_n = heads * dv
    second_local = jnp.concatenate(
        [
            gate_up.reshape(rows, 2 * hidden),
            out_proj.reshape(mix_n, rows).T,
            down_proj.T,
        ],
        1,
    )
    first, second_local = lax.optimization_barrier((first, second_local))
    second = lax.all_gather(second_local, "seq", axis=0, tiled=True)
    gu_full = second[:, : 2 * hidden]
    outp_t = second[:, 2 * hidden : 2 * hidden + mix_n]
    down_t = second[:, 2 * hidden + mix_n :]

    proj_n = qk_n + vg_n + ab_n
    in_proj = first[:, :proj_n]
    norm_float = first[:, proj_n].astype(f32)
    ffng_float = first[:, proj_n + 1].astype(f32)
    small_full = first[:, proj_n + 2 : proj_n + 2 + small_cols].reshape(peers, -1)[:, :small_n]
    qkc_n = taps * 2 * heads * dk_part
    vc_n = taps * heads * dv_part
    qkc_full = jnp.moveaxis(
        small_full[:, :qkc_n].reshape(peers, taps, 2, heads, dk_part), 0, 3
    ).reshape(taps, 2, heads, dk)
    vc_full = jnp.moveaxis(
        small_full[:, qkc_n : qkc_n + vc_n].reshape(peers, taps, heads, dv_part), 0, 2
    ).reshape(taps, heads, dv)
    outg_full = small_full[:, qkc_n + vc_n :].reshape(-1).astype(f32)

    edge_len = taps - 1
    tok_float = tokens.astype(f32)
    tok_rows = head_rows(tokens, quarter).astype(f32)
    cot_rows = head_rows(cotangent, quarter).astype(f32)
    normed_low = input_norm(tok_float, norm_float).astype(bf16)
    pre = jnp.einsum("bld,dn->bln", normed_low, in_proj, preferred_element_type=f32)
    qk_pre = pre[:, :, :qk_n].reshape(seqs, seq_len, 2, heads, dk)
    vg_pre = pre[:, :, qk_n : qk_n + vg_n].reshape(seqs, seq_len, 2, heads, dv)
    ab_pre = pre[:, :, qk_n + vg_n :].reshape(seqs, seq_len, 2, heads)
    edge_n = qk_n + heads * dv
    edge = from_behind(pre[:, seq_len - edge_len :, :edge_n], "seq", 1)
    qk_ext = jnp.concatenate(
        [edge[:, :, :qk_n].reshape(seqs, edge_len, 2, heads, dk), qk_pre], 1
    )
    v_ext = jnp.concatenate(
        [edge[:, :, qk_n:].reshape(seqs, edge_len, heads, dv), vg_pre[:, :, 0]], 1
    )
    span_terms, pull_prepare = jax.vjp(
        prepare, qk_ext, v_ext, ab_pre, qkc_full.astype(f32), vc_full.astype(f32), decay_terms
    )
    whole_map, whole_add = compose(span_terms)
    moved = lax.all_gather(jnp.concatenate([whole_map, whole_add], -1).astype(bf16), "seq")
    moved = moved.astype(f32)
    all_maps, all_adds = moved[..., :dk], moved[..., dk:]
    mine = lax.axis_index("seq")

    def from_first(at, state):
        return jnp.where(at < mine, product(all_maps[at], state) + all_adds[at], state)

    state_in = lax.fori_loop(0, peers - 1, from_first, jnp.zeros_like(whole_add), unroll=peers <= 8)
    mixer_pair, pull_finish = jax.vjp(finish, span_terms, state_in)
    mixer_out = mixer_pair[0]
    gated_out, pull_gate = jax.vjp(output_norm, mixer_out, vg_pre[:, :, 1], outg_full)
    gated_low = gated_out.astype(bf16).reshape(seqs, seq_len, mix_n)
    mix_terms = jnp.einsum("bln,dn->bld", gated_low, outp_t, preferred_element_type=f32)
    mix_rows = lax.psum_scatter(
        mix_terms.astype(bf16), "head", scatter_dimension=1, tiled=True
    )
    hidden_rows = tok_rows + mix_rows.astype(f32)
    normed_ffn, pull_second = jax.vjp(input_norm, hidden_rows, ffng_float)
    normed_ffn_low = lax.all_gather(normed_ffn.astype(bf16), "head", axis=1, tiled=True)
    act_grad = jnp.einsum("bld,df->blf", cotangent, down_t, preferred_element_type=f32)
    gu_pre = jnp.einsum("bld,dn->bln", normed_ffn_low, gu_full, preferred_element_type=f32)
    gu_pre = gu_pre.reshape(seqs, seq_len, 2, hidden)
    activated, pull_swiglu = jax.vjp(swiglu, gu_pre)
    activated_low = activated.astype(bf16)
    gu_grad_low = pull_swiglu(act_grad)[0].astype(bf16).reshape(seqs, seq_len, 2 * hidden)
    ffn_norm_terms = jnp.einsum("bln,dn->bld", gu_grad_low, gu_full, preferred_element_type=f32)
    ffn_norm_rows = lax.psum_scatter(
        ffn_norm_terms.astype(bf16), "head", scatter_dimension=1, tiled=True
    )
    hidden_from_norm, ffn_gain_grad = pull_second(ffn_norm_rows.astype(f32))
    hidden_grad = cot_rows + hidden_from_norm
    mix_grad_low = lax.all_gather(hidden_grad.astype(bf16), "head", axis=1, tiled=True)
    ffn_terms = jnp.einsum("blf,df->bld", activated_low, down_t, preferred_element_type=f32)
    ffn_rows = lax.psum_scatter(
        ffn_terms.astype(bf16), "head", scatter_dimension=1, tiled=True
    )
    block_rows = (hidden_rows + ffn_rows.astype(f32)).astype(bf16)
    block_out = lax.all_gather(block_rows, "head", axis=1, tiled=True)
    down_grad = jnp.einsum("bld,blf->df", cotangent, activated_low, preferred_element_type=f32)
    gu_grad = jnp.einsum("bld,bln->dn", normed_ffn_low, gu_grad_low, preferred_element_type=f32)
    gated_grad = jnp.einsum("bld,dn->bln", mix_grad_low, outp_t, preferred_element_type=f32)
    gated_grad = gated_grad.reshape(seqs, seq_len, heads, dv)
    outp_grad = jnp.einsum("bld,bln->dn", mix_grad_low, gated_low, preferred_element_type=f32)
    second_grad = jnp.concatenate(
        [gu_grad.astype(bf16), outp_grad.astype(bf16), down_grad.astype(bf16)], 1
    )
    second_grad, gated_grad = lax.optimization_barrier((second_grad, gated_grad))
    second_sum = lax.psum_scatter(second_grad, "seq", scatter_dimension=0, tiled=True)
    mixer_grad, gate_grad, out_gain_part = pull_gate(gated_grad)
    carry_map, read_map = (span_terms[0], span_terms[2])
    span_grads = to_spans(mixer_grad)
    read_grads = product(flip(read_map), span_grads)
    state_grad = jnp.zeros_like(whole_add)
    for span_idx in range(carry_map.shape[2] - 1, -1, -1):
        state_grad = read_grads[:, :, span_idx] + product(
            flip(carry_map[:, :, span_idx]), state_grad
        )
    all_grads = lax.all_gather(state_grad.astype(bf16), "seq").astype(f32)

    def from_last(step, state):
        at = peers - 1 - step
        return jnp.where(at > mine, product(flip(all_maps[at]), state) + all_grads[at], state)

    state_out_grad = lax.fori_loop(
        0, peers - 1, from_last, jnp.zeros_like(whole_add), unroll=peers <= 8
    )
    terms_grad, state_in_grad = pull_finish((mixer_grad, state_out_grad))
    qk_ext_grad, v_ext_grad, ab_grad_pre, qk_conv_grad, v_conv_grad, decay_part = pull_prepare(
        terms_grad
    )
    ext_grad = jnp.concatenate(
        [
            qk_ext_grad.reshape(seqs, seq_len + edge_len, qk_n),
            v_ext_grad.reshape(seqs, seq_len + edge_len, heads * dv),
        ],
        2,
    )
    back = from_behind(ext_grad[:, :edge_len], "seq", -1)
    conv_in_grad = ext_grad[:, edge_len:].at[:, seq_len - edge_len :].add(back)
    pre_grad_low = jnp.concatenate(
        [
            conv_in_grad.astype(bf16),
            gate_grad.reshape(seqs, seq_len, heads * dv).astype(bf16),
            ab_grad_pre.reshape(seqs, seq_len, ab_n).astype(bf16),
        ],
        2,
    )
    normed_part = jnp.einsum("bln,dn->bld", pre_grad_low, in_proj, preferred_element_type=f32)
    normed_rows = lax.psum_scatter(
        normed_part.astype(bf16), "head", scatter_dimension=1, tiled=True
    )
    first_grad = jnp.einsum("bld,bln->dn", normed_low, pre_grad_low, preferred_element_type=f32)
    conv_grad = jnp.concatenate(
        [
            jnp.moveaxis(qk_conv_grad.reshape(taps, 2, heads, peers, dk_part), 3, 0).reshape(
                peers, qkc_n
            ),
            jnp.moveaxis(v_conv_grad.reshape(taps, heads, peers, dv_part), 2, 0).reshape(
                peers, vc_n
            ),
        ],
        1,
    )
    conv_n = qkc_n + vc_n
    conv_cols = -(-conv_n // rows)
    conv_grad = jnp.pad(conv_grad, ((0, 0), (0, conv_cols * rows - conv_n)))
    first_grad = jnp.concatenate(
        [
            first_grad.astype(bf16),
            conv_grad.reshape(width, conv_cols).astype(bf16),
            jnp.zeros((width, -(proj_n + conv_cols) % 128), bf16),
        ],
        1,
    )
    first_sum = lax.psum_scatter(first_grad, "seq", scatter_dimension=0, tiled=True).astype(f32)
    _, pull_first = jax.vjp(input_norm, tok_rows, norm_float)
    tok_from_norm, norm_gain_grad = pull_first(normed_rows.astype(f32))
    grad_rows = (hidden_grad + tok_from_norm).astype(bf16)
    tokens_grad = lax.all_gather(grad_rows, "head", axis=1, tiled=True).astype(f32)
    decay_all = lax.dynamic_update_slice(
        jnp.zeros((2, heads * head_peers), f32),
        decay_part,
        (0, lax.axis_index("head") * heads),
    )
    vectors = jnp.concatenate(
        [norm_gain_grad, ffn_gain_grad, out_gain_part, decay_all.reshape(-1)]
    )
    vectors = lax.psum(vectors, ("seq", "head"))
    norm_gain_sum = lax.dynamic_slice_in_dim(vectors, mine * rows, rows, 0)
    ffn_gain_sum = lax.dynamic_slice_in_dim(vectors, width + mine * rows, rows, 0)
    gain_n = out_gain.shape[0]
    out_gain_sum = lax.dynamic_slice_in_dim(vectors, 2 * width + mine * gain_n, gain_n, 0)
    decay_grad = lax.dynamic_slice_in_dim(
        vectors[2 * width + dv :].reshape(2, heads * head_peers),
        lax.axis_index("head") * heads,
        heads,
        1,
    )
    conv_sum = first_sum[:, proj_n : proj_n + conv_cols].reshape(-1)
    second_sum = second_sum.astype(f32)
    return (
        block_out,
        tokens_grad,
        norm_gain_sum,
        first_sum[:, :qk_n].reshape(qk_proj.shape),
        first_sum[:, qk_n : qk_n + vg_n].reshape(vg_proj.shape),
        first_sum[:, qk_n + vg_n : proj_n].reshape(ab_proj.shape),
        conv_sum[:qkc_n].reshape(qk_conv.shape),
        conv_sum[qkc_n:conv_n].reshape(v_conv.shape),
        decay_grad,
        out_gain_sum,
        second_sum[:, 2 * hidden : 2 * hidden + mix_n].T.reshape(out_proj.shape),
        ffn_gain_sum,
        second_sum[:, : 2 * hidden].reshape(gate_up.shape),
        second_sum[:, 2 * hidden + mix_n :].T,
    )


def solution(mesh):
    placed = (
        P(None, "seq", None),
        P("seq"),
        P("seq", None, "head", None),
        P("seq", None, "head", None),
        P("seq", None, "head"),
        P(None, None, "head", "seq"),
        P(None, "head", "seq"),
        P(None, "head"),
        P("seq"),
        P("head", None, "seq"),
        P("seq"),
        P("seq", None, "head"),
        P("head", "seq"),
        P(None, "seq", None),
    )
    return jax.shard_map(
        per_device,
        mesh=mesh,
        in_specs=placed,
        out_specs=(
            P(None, "seq", None),
            P(None, "seq", None),
            P("seq"),
            P("seq", None, "head", None),
            P("seq", None, "head", None),
            P("seq", None, "head"),
            P(None, None, "head", "seq"),
            P(None, "head", "seq"),
            P(None, "head"),
            P("seq"),
            P("head", None, "seq"),
            P("seq"),
            P("seq", None, "head"),
            P("head", "seq"),
        ),
        check_vma=False,
    )
```
